256 devices in a mesh: blk: 32 (over x_hi, z, core), fold: 8 (over x_lo, y).
Axes of the slice: x: 4 (x_hi: 2, x_lo: 2; x = x_hi * 2 + x_lo), y: 4, z: 8, core: 2. Of those that a mesh axis runs over, the one named last changes fastest.
Arguments:
- picture_vectors: bfloat16 [131072, 1152], P(('blk', 'fold')), may hold values from -0.1796875 to 0.1796875
- caption_vectors: bfloat16 [131072, 1152], P(('blk', 'fold')), may hold values from -0.1796875 to 0.1796875
- logit_multiplier: float32 [], replicated, may hold values from 4 to 16
- logit_shift_term: float32 [], replicated, may hold values from -4 to -1
Outputs:
- image_grad: float32 [131072, 1152], P(('blk', 'fold'))
- text_grad: float32 [131072, 1152], P(('blk', 'fold'))
The draws below stay inside these ranges and needn't reach their ends.
All inputs are finite; a program needn't handle non-finite values.
Results may differ from the reference program's by a relative error of at most 0.013.
Values may be sent and summed in bfloat16 or wider, within the bound.
A program may use at most 64 MiB of HBM per device.

```python
import math
import jax
import jax.numpy as jnp
from jax import lax

D = 1152
ROWS = 512
STEPS = 4
BATCH = 131072


def shard_levels(key, extent, shards, smallest, top_value):
    loudness = 1.0
    for dim, parts in shards:
        heights = jax.random.uniform(jax.random.fold_in(jax.random.fold_in(key, 6), dim), (parts,), jnp.float32, smallest / len(shards), top_value / len(shards))
        loudness = loudness * jnp.repeat(jnp.exp(heights), extent[dim] // parts).reshape((-1,) + (1,) * (len(extent) - 1 - dim))
    return loudness


def normal_values(key, extent, scale, limit, shards=(), kind=jnp.bfloat16):
    values = jax.random.normal(key, extent, jnp.float32) * scale
    if len(shards) > 0:
        values = shard_levels(key, extent, shards, -0.22, 0.18) * values
    return jnp.clip(values, min=-limit, max=limit).astype(kind)


def setup_inputs(seed: int = 0) -> dict:
    streams_of = jax.random.split(jax.random.key(seed), 5)
    picture_vectors = normal_values(streams_of[0], (BATCH, D), 0.03, 0.1796875, ((0, 256),))
    caption_vectors = normal_values(streams_of[1], (BATCH, D), 0.03, 0.1796875, ((0, 256),))
    logit_multiplier = jnp.clip(jnp.exp(jax.random.uniform(streams_of[2], (), jnp.float32, math.log(4.0), math.log(16.0))), 4.0, 16.0)
    logit_shift_term = jnp.clip(jax.random.uniform(streams_of[3], (), jnp.float32, -4.0, -1.0), -4.0, -1.0)
    return dict(picture_vectors=picture_vectors, caption_vectors=caption_vectors, logit_multiplier=logit_multiplier, logit_shift_term=logit_shift_term)


def unit_rows(raw):
    wide = raw.astype(jnp.float32)
    scale = 1.0 / jnp.sqrt(lax.optimization_barrier(jnp.sum(wide * wide, axis=-1, keepdims=True)) + 1e-06)
    return (scale, wide * scale)

def back_rows(scale, unit, grad):
    inner = lax.optimization_barrier(jnp.sum(unit * grad, axis=-1, keepdims=True))
    return scale * (grad - unit * inner)

def reference(picture_vectors, caption_vectors, logit_multiplier, logit_shift_term):
    blocks = BATCH // ROWS
    image_scale, image_unit = unit_rows(picture_vectors)
    text_scale, text_unit = unit_rows(caption_vectors)
    picture_direction = image_unit.astype(jnp.bfloat16).reshape(blocks, ROWS, D).astype(jnp.float32)
    text_hat = text_unit.astype(jnp.bfloat16).reshape(blocks, ROWS, D).astype(jnp.float32)
    identity = jnp.eye(ROWS, dtype=jnp.float32)
    hat_image = jnp.zeros((blocks, ROWS, D), jnp.float32)
    hat_text = jnp.zeros((blocks, ROWS, D), jnp.float32)
    for shift_step in range(STEPS):
        counterpart_tile = jnp.roll(text_hat, shift_step, axis=0)
        similarity_scores = logit_multiplier * jnp.einsum('ruk,rtk->rut', picture_direction, counterpart_tile) + logit_shift_term
        target_signs = identity if shift_step == 0 else jnp.zeros_like(identity)
        objective_weight = (logit_multiplier * (jax.nn.sigmoid(similarity_scores) - target_signs)).astype(jnp.bfloat16).astype(jnp.float32)
        hat_image = hat_image + jnp.einsum('bij,bjd->bid', objective_weight, counterpart_tile)
        contrib = jnp.einsum('bij,bid->bjd', objective_weight, picture_direction)
        hat_text = hat_text + jnp.roll(contrib, -shift_step, axis=0)
    image_grad = back_rows(image_scale, image_unit, hat_image.reshape(BATCH, D))
    text_grad = back_rows(text_scale, text_unit, hat_text.reshape(BATCH, D))
    return (image_grad, text_grad)
```

```python
import functools

import jax
import jax.numpy as jnp
from jax import lax
from jax.experimental import pallas as pl
from jax.experimental.pallas import tpu as pltpu
from jax.sharding import PartitionSpec as P

MESH = pl.DeviceIdType.MESH
PIECES = 8
PARTS = 4
OWN, PARTNER = 0, 1
A, M, X = 0, 1, 2


def kernel(
    total, fold_size, image_ref, text_ref, mult_ref, shift_ref, image_out, text_out,
    raw, imgs, texts, scales, gi, gt, gp_out, gm_out, gx_out, gp_in, gm_in, gx_in, stage,
    load_sem, store_sem, i_send, i_recv, m_send, m_recv, x_send, x_recv,
    gp_send, gp_recv, gm_send, gm_recv, gx_send, gx_recv,
):
    rows, width = raw.shape[1:]
    piece, part = rows // PIECES, rows // PARTS
    per = PIECES // PARTS
    d = lax.axis_index("blk") * fold_size + lax.axis_index("fold")
    y = lax.rem(d, 4)
    odd = lax.rem(y, 2)
    mult, shift = mult_ref[0, 0], shift_ref[0, 0]

    def device(number):
        number = lax.rem(number + total, total)
        return (number // fold_size, lax.rem(number, fold_size))

    def where(*values):
        picked = jnp.int32(values[0])
        for place in range(1, 4):
            picked = jnp.where(y == place, jnp.int32(values[place]), picked)
        return picked

    def among(*places):
        met = y == places[0]
        for place in places[1:]:
            met = jnp.logical_or(met, y == place)
        return met

    def span(f, size=None):
        size = piece if size is None else size
        return pl.ds(pl.multiple_of(f * size, size), size)

    partner = device(d + 1 - 2 * odd)
    m_target = device(d + where(3, 1, 3, -3))
    gm_target = device(d + where(3, 1, -1, -3))

    def remote(src, dst, send, recv, f, target):
        return pltpu.make_async_remote_copy(
            src_ref=src, dst_ref=dst, send_sem=send.at[f], recv_sem=recv.at[f],
            device_id=target, device_id_type=MESH,
        )

    def i_copy(f):
        return remote(imgs.at[OWN, span(f)], imgs.at[PARTNER, span(f)], i_send, i_recv, f, partner)

    def m_copy(f, slot):
        return remote(texts.at[slot, span(f)], texts.at[M, span(f)], m_send, m_recv, f, m_target)

    def x_copy(f):
        return remote(texts.at[A, span(f)], texts.at[X, span(f)], x_send, x_recv, f, device(d + 4))

    def gp_copy(f):
        return remote(gp_out.at[span(f)], gp_in.at[span(f)], gp_send, gp_recv, f, partner)

    def gm_copy(f):
        return remote(gm_out.at[span(f)], gm_in.at[span(f)], gm_send, gm_recv, f, gm_target)

    def gx_copy(f, source):
        return remote(source.at[span(f)], gx_in.at[span(f)], gx_send, gx_recv, f, device(d - 4))

    def load(which, f):
        source = (image_ref, text_ref)[which]
        return pltpu.make_async_copy(
            source.at[span(f)], raw.at[which, span(f)], load_sem.at[which, f]
        )

    barrier = pltpu.get_barrier_semaphore()
    near = {0: (1, 3), 1: (-1, 1, 4, -4, -3), 2: (1, 3, -1, 4, -4), 3: (-1, -3, 4, -4)}
    for f in range(PIECES):
        load(0, f).start()
        load(1, f).start()
    for place, offsets in near.items():

        @pl.when(y == place)
        def _():
            for offset in offsets:
                pl.semaphore_signal(
                    barrier, inc=1, device_id=device(d + offset), device_id_type=MESH
                )

    def normalize(which, f):
        load(which, f).wait()
        wide = raw[which, span(f), :].astype(jnp.float32)
        scale = 1.0 / jnp.sqrt(jnp.sum(wide * wide, axis=-1, keepdims=True) + 1e-06)
        scales[which, span(f), :] = jnp.broadcast_to(scale, (piece, scales.shape[-1]))
        (imgs, texts)[which][0, span(f), :] = (wide * scale).astype(jnp.bfloat16)

    normalize(0, 0)
    normalize(1, 0)
    for place, offsets in near.items():

        @pl.when(y == place)
        def _():
            pl.semaphore_wait(barrier, len(offsets))

    def send_in(f):
        i_copy(f).start()

        @pl.when(y < 3)
        def _():
            m_copy(f, A).start()

        @pl.when(odd == 1)
        def _():
            x_copy(f).start()

    send_in(0)

    @pl.loop(1, PIECES)
    def _(f):
        normalize(0, f)
        normalize(1, f)
        send_in(f)

    def forward(f):
        @pl.when(y == 3)
        def _():
            x_copy(f).wait_recv()
            m_copy(f, X).start()

    def tile(image, i0, i_rows, text, t0, t_rows, diagonal=False, fresh=False):
        pictures = imgs[image, pl.ds(i0, i_rows), :]
        captions = texts[text, pl.ds(t0, t_rows), :]
        scores = lax.dot_general(
            pictures, captions, (((1,), (1,)), ((), ())), preferred_element_type=jnp.float32
        )
        weights = jax.nn.sigmoid(mult * scores + shift)
        if diagonal:
            r = lax.broadcasted_iota(jnp.int32, weights.shape, 0) + i0
            c = lax.broadcasted_iota(jnp.int32, weights.shape, 1) + t0
            weights = jnp.where(r == c, weights - 1.0, weights)
        coeff = (mult * weights).astype(jnp.bfloat16)
        to_image = jnp.dot(coeff, captions, preferred_element_type=jnp.float32)
        to_text = lax.dot_general(
            coeff, pictures, (((0,), (0,)), ((), ())), preferred_element_type=jnp.float32
        )
        if fresh:
            gi[image, pl.ds(i0, i_rows), :] = to_image
        else:
            gi[image, pl.ds(i0, i_rows), :] += to_image
        gt[text, pl.ds(t0, t_rows), :] += to_text

    def at(c):
        return pl.multiple_of(c * part, part)

    forward(0)
    gt[...] = jnp.zeros_like(gt)
    gi[PARTNER] = jnp.zeros_like(gi[PARTNER])

    @pl.loop(0, PARTS)
    def _(c):
        tile(OWN, at(c), part, A, 0, rows, diagonal=True, fresh=True)

    def corner(text, c):
        @pl.loop(0, c)
        def _(k):
            tile(PARTNER, at(k), part, text, at(c), part)

        @pl.loop(0, c + 1)
        def _(k):
            tile(PARTNER, at(c), part, text, at(k), part)

    def arrived(f, with_x):
        i_copy(f).wait_recv()
        m_copy(f, A).wait_recv()
        if with_x:

            @pl.when(y == 1)
            def _():
                x_copy(f).wait_recv()

    def own_with_m(c):
        tile(OWN, 0, rows, M, at(c), part)

    for c in range(PARTS - 1):
        for f in range(c * per, (c + 1) * per):
            if f > 0:
                forward(f)
        for f in range(c * per, (c + 1) * per):
            arrived(f, True)
        own_with_m(c)
        corner(M, c)

        @pl.when(odd == 0)
        def _():
            tile(PARTNER, at(c), part, A, 0, rows)

        @pl.when(odd == 1)
        def _():
            corner(X, c)

    last = PARTS - 1
    for f in range(last * per, PIECES):
        forward(f)
    for f in range(last * per, PIECES):
        arrived(f, True)

    def send_back(grad, out, copy, c):
        out[span(c, part), :] = grad[span(c, part), :].astype(jnp.bfloat16)
        for f in range(per):
            copy(c * per + f).start()

    def give_gp(c):
        send_back(gi.at[PARTNER], gp_out, gp_copy, c)

    def give_gm(c):
        send_back(gt.at[M], gm_out, gm_copy, c)

    def give_gx(c):
        @pl.when(y == 1)
        def _():
            send_back(gt.at[X], gx_out, lambda f: gx_copy(f, gx_out), c)

    @pl.loop(0, last)
    def _(k):
        tile(PARTNER, at(k), part, M, at(last), part)

        @pl.when(odd == 1)
        def _():
            tile(PARTNER, at(k), part, X, at(last), part)

        give_gp(k)
        tile(PARTNER, at(last), part, M, at(k), part)
        give_gm(k)

        @pl.when(odd == 1)
        def _():
            tile(PARTNER, at(last), part, X, at(k), part)

        give_gx(k)

    tile(PARTNER, at(last), part, M, at(last), part)

    @pl.when(odd == 0)
    def _():
        tile(PARTNER, at(last), part, A, 0, rows)

    @pl.when(odd == 1)
    def _():
        tile(PARTNER, at(last), part, X, at(last), part)

    give_gp(last)
    give_gx(last)
    own_with_m(last)
    give_gm(last)

    def store(which, f):
        target = (image_out, text_out)[which]
        slot = lax.rem(f, 2)
        return pltpu.make_async_copy(
            stage.at[which, slot], target.at[span(f)], store_sem.at[which, slot]
        )

    def finish(which, f, grad):
        scale = scales[which, span(f), :][:, :1]
        unit = raw[which, span(f), :].astype(jnp.float32) * scale
        inner = jnp.sum(unit * grad, axis=-1, keepdims=True)

        @pl.when(f >= 2)
        def _():
            store(which, f - 2).wait()

        stage[which, lax.rem(f, 2)] = scale * (grad - unit * inner)
        store(which, f).start()

    def wide(ref, f):
        return ref[span(f), :].astype(jnp.float32)

    def relay(f):
        @pl.when(y == 2)
        def _():
            gm_copy(f).wait_recv()
            gx_copy(f, gm_in).start()

        @pl.when(y == 3)
        def _():
            gm_copy(f).wait_recv()
            gx_out[span(f), :] = (gt[X, span(f), :] + wide(gm_in, f)).astype(jnp.bfloat16)
            gx_copy(f, gx_out).start()

    def finish_image(f):
        gp_copy(f).wait_recv()
        finish(0, f, gi[OWN, span(f), :] + wide(gp_in, f))

    def finish_text(f):
        @pl.when(y < 2)
        def _():
            gm_copy(f).wait_recv()
            gt[A, span(f), :] += wide(gm_in, f)

        @pl.when(y > 0)
        def _():
            gx_copy(f, gx_out).wait_recv()
            gt[A, span(f), :] += wide(gx_in, f)

        finish(1, f, gt[A, span(f), :])

    @pl.loop(0, PIECES)
    def _(f):
        relay(f)
        finish_image(f)

        @pl.when(f >= 1)
        def _():
            finish_text(f - 1)

    finish_text(PIECES - 1)

    @pl.loop(0, PIECES)
    def _(f):
        i_copy(f).wait_send()
        m_copy(f, A).wait_send()
        gp_copy(f).wait_send()
        gm_copy(f).wait_send()

        @pl.when(odd == 1)
        def _():
            x_copy(f).wait_send()

        @pl.when(y > 0)
        def _():
            gx_copy(f, gx_out).wait_send()

    for f in range(PIECES - 2, PIECES):
        store(0, f).wait()
        store(1, f).wait()


def solution(mesh):
    fold_size = mesh.shape["fold"]
    total = fold_size * mesh.shape["blk"]

    def shards(picture_vectors, caption_vectors, logit_multiplier, logit_shift_term):
        rows, width = picture_vectors.shape
        block = (rows, width)
        dma = pltpu.SemaphoreType.DMA
        return pl.pallas_call(
            functools.partial(kernel, total, fold_size),
            out_shape=(jax.ShapeDtypeStruct(block, jnp.float32),) * 2,
            in_specs=[pl.BlockSpec(memory_space=pl.ANY)] * 2
            + [pl.BlockSpec(memory_space=pltpu.SMEM)] * 2,
            out_specs=(pl.BlockSpec(memory_space=pl.ANY),) * 2,
            scratch_shapes=[
                pltpu.VMEM((2,) + block, jnp.bfloat16),
                pltpu.VMEM((2,) + block, jnp.bfloat16),
                pltpu.VMEM((3,) + block, jnp.bfloat16),
                pltpu.VMEM((2, rows, 128), jnp.float32),
                pltpu.VMEM((2,) + block, jnp.float32),
                pltpu.VMEM((3,) + block, jnp.float32),
                pltpu.VMEM(block, jnp.bfloat16),
                pltpu.VMEM(block, jnp.bfloat16),
                pltpu.VMEM(block, jnp.bfloat16),
                pltpu.VMEM(block, jnp.bfloat16),
                pltpu.VMEM(block, jnp.bfloat16),
                pltpu.VMEM(block, jnp.bfloat16),
                pltpu.VMEM((2, 2, rows // PIECES, width), jnp.float32),
                dma((2, PIECES)),
                dma((2, 2)),
            ]
            + [dma((PIECES,))] * 12,
            compiler_params=pltpu.CompilerParams(
                collective_id=0, has_side_effects=True, vmem_limit_bytes=48 << 20
            ),
            cost_estimate=pl.CostEstimate(
                flops=24 * rows * rows * width,
                bytes_accessed=12 * rows * width,
                transcendentals=4 * rows * rows,
            ),
        )(
            picture_vectors,
            caption_vectors,
            logit_multiplier.reshape(1, 1),
            logit_shift_term.reshape(1, 1),
        )

    placed = (P(("blk", "fold"), None), P(("blk", "fold"), None), P(), P())
    return jax.shard_map(
        shards,
        mesh=mesh,
        in_specs=placed,
        out_specs=(P(("blk", "fold"), None), P(("blk", "fold"), None)),
        check_vma=False,
    )
```

```python
import functools

import jax
import jax.numpy as jnp
from jax import lax
from jax.experimental import pallas as pl
from jax.experimental.pallas import tpu as pltpu
from jax.sharding import PartitionSpec as P

MESH = pl.DeviceIdType.MESH
PIECES = 8
PARTS = 4
HALVES = 2
OWN, PARTNER = 0, 1
A, M, X = 0, 1, 2


def kernel(
    total, fold_size, image_ref, text_ref, mult_ref, shift_ref, image_out, text_out,
    raw, imgs, texts, passing, scales, c_oa, c_px, c_om, c_pm, gi, gt, gx,
    gp_out, gm_out, gx_out, gp_in, gm_in, gx_in, stage,
    load_sem, store_sem, i_send, i_recv, m_send, m_recv, x_send, x_recv, r_send, r_recv, fw_send,
    gp_send, gp_recv, gm_send, gm_recv, gx_send, gx_recv,
):
    rows, width = raw.shape[1:]
    piece, part, half = rows // PIECES, rows // PARTS, rows // HALVES
    low = PIECES // HALVES
    per = PIECES // PARTS
    d = lax.axis_index("blk") * fold_size + lax.axis_index("fold")
    y = lax.rem(d, 4)
    odd = lax.rem(y, 2)
    x_slot = 2 * odd
    mult, shift = mult_ref[0, 0], shift_ref[0, 0]

    def device(number):
        number = lax.rem(number + total, total)
        return (number // fold_size, lax.rem(number, fold_size))

    def where(*values):
        picked = jnp.int32(values[0])
        for place in range(1, 4):
            picked = jnp.where(y == place, jnp.int32(values[place]), picked)
        return picked

    def span(f, size=None):
        size = piece if size is None else size
        return pl.ds(pl.multiple_of(f * size, size), size)

    partner = device(d + 1 - 2 * odd)

    def remote(src, dst, send, recv, target):
        return pltpu.make_async_remote_copy(
            src_ref=src, dst_ref=dst, send_sem=send, recv_sem=recv,
            device_id=target, device_id_type=MESH,
        )

    def i_copy(f):
        return remote(
            imgs.at[OWN, span(f)], imgs.at[PARTNER, span(f)], i_send.at[f], i_recv.at[f], partner
        )

    def m_copy(f, slot=A):
        return remote(
            texts.at[slot, span(f)], texts.at[M, span(f)], m_send.at[f], m_recv.at[f],
            device(d + where(3, 1, 3, -3)),
        )

    def x_copy(f):
        return remote(
            texts.at[A, span(f)], texts.at[X, span(f)], x_send.at[f], x_recv.at[f], device(d + 4)
        )

    def r_copy(f):
        return remote(
            texts.at[A, span(f)], passing.at[span(f)], r_send.at[f], r_recv.at[f], device(d - 3)
        )

    def r_forward(f):
        return remote(
            passing.at[span(f)], texts.at[M, span(f)], fw_send.at[f], m_recv.at[f], device(d + 4)
        )

    def gp_copy(f):
        return remote(gp_out.at[span(f)], gp_in.at[span(f)], gp_send.at[f], gp_recv.at[f], partner)

    def gm_copy(f):
        step = where(3, 1, -1, -3)
        step = jnp.where(jnp.logical_and(y == 0, f >= low), -1, step)
        return remote(
            gm_out.at[span(f)], gm_in.at[span(f)], gm_send.at[f], gm_recv.at[f], device(d + step)
        )

    def gx_copy(f, source):
        return remote(
            source.at[span(f)], gx_in.at[span(f)], gx_send.at[f], gx_recv.at[f], device(d - 4)
        )

    def load(which, f):
        source = (image_ref, text_ref)[which]
        return pltpu.make_async_copy(
            source.at[span(f)], raw.at[which, span(f)], load_sem.at[which, f]
        )

    barrier = pltpu.get_barrier_semaphore()
    near = {0: (1, 3, 4, -4, -1), 1: (-1, 1, 4, -4, -3), 2: (1, 3, -1, 4, -4), 3: (-1, -3, 4, -4, 1)}
    for place, offsets in near.items():

        @pl.when(y == place)
        def _():
            for offset in offsets:
                pl.semaphore_signal(
                    barrier, inc=1, device_id=device(d + offset), device_id_type=MESH
                )

    for f in range(PIECES):
        load(0, f).start()
        load(1, f).start()

    def normalize(which, f):
        load(which, f).wait()
        wide = raw[which, span(f), :].astype(jnp.float32)
        scale = 1.0 / jnp.sqrt(jnp.sum(wide * wide, axis=-1, keepdims=True) + 1e-06)
        scales[which, span(f), :] = jnp.broadcast_to(scale, (piece, scales.shape[-1]))
        (imgs, texts)[which][0, span(f), :] = (wide * scale).astype(jnp.bfloat16)

    def x_piece(f):
        return lax.rem(f + low, PIECES)

    def send_text(f):
        @pl.when(y < 3)
        def _():
            m_copy(f).start()

        @pl.when(jnp.logical_and(y == 3, f < low))
        def _():
            r_copy(f).start()

    normalize(0, 0)
    normalize(1, 0)
    pl.semaphore_wait(barrier, 5)
    i_copy(0).start()
    send_text(jnp.int32(0))

    @pl.loop(1, low)
    def _(f):
        normalize(0, f)
        normalize(1, f)
        i_copy(f).start()
        send_text(f)

    @pl.loop(low, PIECES)
    def _(f):
        normalize(1, f)
        send_text(f)

        @pl.when(odd == 1)
        def _():
            x_copy(f).start()

        normalize(0, f)
        i_copy(f).start()

    @pl.when(odd == 1)
    def _():
        for f in range(low):
            x_copy(f).start()

    def weigh(c_ref, image, i0, i_rows, text, t0, t_rows, diagonal=False):
        scores = lax.dot_general(
            imgs[image, pl.ds(i0, i_rows), :], texts[text, pl.ds(t0, t_rows), :],
            (((1,), (1,)), ((), ())), preferred_element_type=jnp.float32,
        )
        weights = jax.nn.sigmoid(mult * scores + shift)
        if diagonal:
            r = lax.broadcasted_iota(jnp.int32, weights.shape, 0) + i0
            c = lax.broadcasted_iota(jnp.int32, weights.shape, 1) + t0
            weights = jnp.where(r == c, weights - 1.0, weights)
        c_ref[pl.ds(i0, i_rows), pl.ds(t0, t_rows)] = (mult * weights).astype(jnp.bfloat16)

    def to_image(c_ref, c, text):
        return jnp.dot(
            c_ref[span(c, part), :], texts[text], preferred_element_type=jnp.float32
        )

    def to_text(c_ref, c, image):
        return lax.dot_general(
            c_ref[:, c * part : (c + 1) * part], imgs[image], (((0,), (0,)), ((), ())),
            preferred_element_type=jnp.float32,
        )

    weigh(c_oa, OWN, 0, half, A, 0, rows, diagonal=True)
    weigh(c_oa, OWN, half, half, A, 0, rows, diagonal=True)
    for c in range(PARTS):
        gi[span(c, part), :] = to_image(c_oa, c, A)
    for c in range(PARTS):
        gt[span(c, part), :] = to_text(c_oa, c, OWN)

    @pl.when(y == 0)
    def _():
        @pl.loop(0, low)
        def _(f):
            r_copy(f).wait_recv()
            r_forward(f).start()

    @pl.when(y == 3)
    def _():
        @pl.loop(0, low)
        def _(f):
            r_copy(f).wait_send()
            x_copy(f + low).wait_recv()
            m_copy(f + low, X).start()

    @pl.when(y == 1)
    def _():
        @pl.loop(low, PIECES)
        def _(f):
            x_copy(f).wait_recv()

    def wait_pair(first, past):
        @pl.loop(first, past)
        def _(f):
            i_copy(f).wait_recv()
            m_copy(f).wait_recv()

    wait_pair(0, low)
    weigh(c_om, OWN, 0, rows, M, 0, half)
    weigh(c_pm, PARTNER, 0, half, M, 0, half)
    weigh(c_px, PARTNER, 0, half, x_slot, half, half)

    wait_pair(low, PIECES)

    @pl.when(odd == 1)
    def _():
        @pl.loop(0, low)
        def _(f):
            x_copy(f).wait_recv()

    def give(value, out, copy, c):
        out[span(c, part), :] = value.astype(jnp.bfloat16)
        for f in range(c * per, (c + 1) * per):
            copy(f).start()

    def give_gp(c):
        give(to_image(c_px, c, x_slot) + to_image(c_pm, c, M), gp_out, gp_copy, c)

    def give_gm(c):
        give(to_text(c_om, c, OWN) + to_text(c_pm, c, PARTNER), gm_out, gm_copy, c)

    def give_gx(c):
        gx[span(c, part), :] = to_text(c_px, c, PARTNER)

        @pl.when(jnp.logical_or(y == 1, y == 3) if c >= PARTS // 2 else y == 1)
        def _():
            give(gx[span(c, part), :], gx_out, lambda f: gx_copy(f, gx_out), c)

    weigh(c_pm, PARTNER, half, half, M, 0, half)
    give_gm(0)
    weigh(c_pm, PARTNER, 0, half, M, half, half)
    weigh(c_px, PARTNER, 0, half, x_slot, 0, half)
    give_gp(0)
    give_gm(1)
    give_gp(1)
    weigh(c_px, PARTNER, half, half, x_slot, half, half)
    give_gx(2)
    give_gx(3)
    weigh(c_px, PARTNER, half, half, x_slot, 0, half)
    weigh(c_pm, PARTNER, half, half, M, half, half)
    weigh(c_om, OWN, 0, rows, M, half, half)
    give_gm(2)
    give_gp(2)
    give_gm(3)
    give_gp(3)
    give_gx(0)
    give_gx(1)

    def wide(ref, f):
        return ref[span(f), :].astype(jnp.float32)

    def relay(f):
        @pl.when(y == 2)
        def _():
            gm_copy(f).wait_recv()
            gx_copy(f, gm_in).start()

        @pl.when(jnp.logical_and(y == 3, f < low))
        def _():
            gm_copy(f).wait_recv()
            gx_out[span(f), :] = (gx[span(f), :] + wide(gm_in, f)).astype(jnp.bfloat16)
            gx_copy(f, gx_out).start()

    for c in range(PARTS):
        relay(jnp.int32(c))
        gi[span(c, part), :] += to_image(c_om, c, M)

        @pl.when(odd == 0)
        def _():
            gt[span(c, part), :] += gx[span(c, part), :]

    def store(which, f):
        target = (image_out, text_out)[which]
        slot = lax.rem(f, 2)
        return pltpu.make_async_copy(
            stage.at[which, slot], target.at[span(f)], store_sem.at[which, slot]
        )

    def finish(which, f, grad):
        scale = scales[which, span(f), :][:, :1]
        unit = raw[which, span(f), :].astype(jnp.float32) * scale
        inner = jnp.sum(unit * grad, axis=-1, keepdims=True)

        @pl.when(f >= 2)
        def _():
            store(which, f - 2).wait()

        stage[which, lax.rem(f, 2)] = scale * (grad - unit * inner)
        store(which, f).start()

    def finish_image(f):
        gp_copy(f).wait_recv()
        finish(0, f, gi[span(f), :] + wide(gp_in, f))

    def finish_text(f):
        @pl.when(jnp.logical_or(y < 2, jnp.logical_and(y == 3, f >= low)))
        def _():
            gm_copy(f).wait_recv()
            gt[span(f), :] += wide(gm_in, f)

        @pl.when(y > 0)
        def _():
            gx_copy(f, gx_out).wait_recv()
            gt[span(f), :] += wide(gx_in, f)

        finish(1, f, gt[span(f), :])

    @pl.loop(0, PIECES)
    def _(f):
        @pl.when(f >= PARTS)
        def _():
            relay(f)

        finish_image(f)

        @pl.when(f >= 1)
        def _():
            finish_text(f - 1)

    finish_text(jnp.int32(PIECES - 1))

    @pl.loop(0, PIECES)
    def _(f):
        i_copy(f).wait_send()
        gp_copy(f).wait_send()
        gm_copy(f).wait_send()

        @pl.when(jnp.logical_or(y < 3, f >= low))
        def _():
            m_copy(f).wait_send()

        @pl.when(jnp.logical_and(y == 0, f < low))
        def _():
            r_forward(f).wait_send()

        @pl.when(odd == 1)
        def _():
            x_copy(f).wait_send()

        @pl.when(y > 0)
        def _():
            gx_copy(f, gx_out).wait_send()

    for f in range(PIECES - 2, PIECES):
        store(0, jnp.int32(f)).wait()
        store(1, jnp.int32(f)).wait()


def solution(mesh):
    fold_size = mesh.shape["fold"]
    total = fold_size * mesh.shape["blk"]

    def shards(picture_vectors, caption_vectors, logit_multiplier, logit_shift_term):
        rows, width = picture_vectors.shape
        block = (rows, width)
        dma = pltpu.SemaphoreType.DMA
        return pl.pallas_call(
            functools.partial(kernel, total, fold_size),
            out_shape=(jax.ShapeDtypeStruct(block, jnp.float32),) * 2,
            in_specs=[pl.BlockSpec(memory_space=pl.ANY)] * 2
            + [pl.BlockSpec(memory_space=pltpu.SMEM)] * 2,
            out_specs=(pl.BlockSpec(memory_space=pl.ANY),) * 2,
            scratch_shapes=[
                pltpu.VMEM((2,) + block, jnp.bfloat16),
                pltpu.VMEM((2,) + block, jnp.bfloat16),
                pltpu.VMEM((3,) + block, jnp.bfloat16),
                pltpu.VMEM((rows // HALVES, width), jnp.bfloat16),
                pltpu.VMEM((2, rows, 128), jnp.float32),
            ]
            + [pltpu.VMEM((rows, rows), jnp.bfloat16)] * 4
            + [pltpu.VMEM(block, jnp.float32)] * 3
            + [pltpu.VMEM(block, jnp.bfloat16)] * 6
            + [
                pltpu.VMEM((2, 2, rows // PIECES, width), jnp.float32),
                dma((2, PIECES)),
                dma((2, 2)),
            ]
            + [dma((PIECES,))] * 15,
            compiler_params=pltpu.CompilerParams(
                collective_id=0, has_side_effects=True, vmem_limit_bytes=58 << 20
            ),
            cost_estimate=pl.CostEstimate(
                flops=24 * rows * rows * width,
                bytes_accessed=12 * rows * width,
                transcendentals=4 * rows * rows,
            ),
        )(
            picture_vectors,
            caption_vectors,
            logit_multiplier.reshape(1, 1),
            logit_shift_term.reshape(1, 1),
        )

    placed = (P(("blk", "fold"), None), P(("blk", "fold"), None), P(), P())
    return jax.shard_map(
        shards,
        mesh=mesh,
        in_specs=placed,
        out_specs=(P(("blk", "fold"), None), P(("blk", "fold"), None)),
        check_vma=False,
    )
```

```python
import functools

import jax
import jax.numpy as jnp
from jax import lax
from jax.experimental import pallas as pl
from jax.experimental.pallas import tpu as pltpu
from jax.sharding import PartitionSpec as P

MESH = pl.DeviceIdType.MESH
PIECES = 8
PARTS = 4
LATE = 7
HALVES = 2
OWN, PARTNER = 0, 1
A, M, X = 0, 1, 2


def kernel(
    total, fold_size, image_ref, text_ref, mult_ref, shift_ref, image_out, text_out,
    raw, imgs, texts, passing, scales, c_oa, c_px, c_om, c_pm, gi, gt, early_m, early_x, early_p,
    gp_out, gm_out, gx_out, gp_in, gm_in, gx_in,
    load_sem, i_send, i_recv, m_send, m_recv, x_send, x_recv, r_send, r_recv, fw_send,
    gp_send, gp_recv, gm_send, gm_recv, gx_send, gx_recv,
):
    rows, width = raw.shape[1:]
    piece, part, half = rows // PIECES, rows // PARTS, rows // HALVES
    low = PIECES // HALVES
    low_part = PARTS // HALVES
    per = PIECES // PARTS
    d = lax.axis_index("blk") * fold_size + lax.axis_index("fold")
    y = lax.rem(d, 4)
    odd = lax.rem(y, 2)
    x_slot = 2 * odd
    mult, shift = mult_ref[0, 0], shift_ref[0, 0]

    def device(number):
        number = lax.rem(number + total, total)
        return (number // fold_size, lax.rem(number, fold_size))

    def where(*values):
        picked = jnp.int32(values[0])
        for place in range(1, 4):
            picked = jnp.where(y == place, jnp.int32(values[place]), picked)
        return picked

    def span(f, size=None):
        size = piece if size is None else size
        return pl.ds(pl.multiple_of(f * size, size), size)

    partner = device(d + 1 - 2 * odd)

    def remote(src, dst, send, recv, target):
        return pltpu.make_async_remote_copy(
            src_ref=src, dst_ref=dst, send_sem=send, recv_sem=recv,
            device_id=target, device_id_type=MESH,
        )

    def i_copy(f):
        return remote(
            imgs.at[OWN, span(f, part)], imgs.at[PARTNER, span(f, part)], i_send.at[f], i_recv.at[f], partner
        )

    def m_copy(f, slot=A):
        return remote(
            texts.at[slot, span(f, part)], texts.at[M, span(f, part)], m_send.at[f], m_recv.at[f],
            device(d + where(3, 1, 3, -3)),
        )

    def x_copy(f):
        return remote(
            texts.at[A, span(f, part)], texts.at[X, span(f, part)], x_send.at[f], x_recv.at[f], device(d + 4)
        )

    def r_copy(f):
        return remote(
            texts.at[A, span(f, part)], passing.at[span(f, part)], r_send.at[f], r_recv.at[f], device(d - 3)
        )

    def r_forward(f):
        return remote(
            passing.at[span(f, part)], texts.at[M, span(f, part)], fw_send.at[f], m_recv.at[f], device(d + 4)
        )

    def gp_copy(f):
        return remote(gp_out.at[span(f, part)], gp_in.at[span(f, part)], gp_send.at[f], gp_recv.at[f], partner)

    straight = where(low, LATE, PIECES, PIECES)
    straight_in = where(PIECES, PIECES, LATE, low)

    def gm_copy(f):
        step = jnp.where(f >= straight, where(-1, -3, -1, -3), where(3, 1, -1, -3))
        return remote(
            gm_out.at[span(f)], gm_in.at[span(f)], gm_send.at[f], gm_recv.at[f], device(d + step)
        )

    def gx_copy(f, source):
        return remote(
            source.at[span(f)], gx_in.at[span(f)], gx_send.at[f], gx_recv.at[f], device(d - 4)
        )

    def load(which, f):
        source = (image_ref, text_ref)[which]
        return pltpu.make_async_copy(
            source.at[span(f, part)], raw.at[which, span(f, part)], load_sem.at[which, f]
        )

    barrier = pltpu.get_barrier_semaphore()
    near = {0: (1, 3, 4, -4, -1), 1: (-1, 1, 4, -4, -3), 2: (1, 3, -1, 4, -4), 3: (-1, -3, 4, -4, 1)}
    for place, offsets in near.items():

        @pl.when(y == place)
        def _():
            for offset in offsets:
                pl.semaphore_signal(
                    barrier, inc=1, device_id=device(d + offset), device_id_type=MESH
                )

    for f in range(PARTS):
        load(0, f).start()
        load(1, f).start()

    def normalize(which, f):
        load(which, f).wait()
        here = span(f, part)
        wide = raw[which, here, :].astype(jnp.float32)
        scale = 1.0 / jnp.sqrt(jnp.sum(wide * wide, axis=-1, keepdims=True) + 1e-06)
        scales[which, here, :] = jnp.broadcast_to(scale, (part, scales.shape[-1]))
        (imgs, texts)[which][0, here, :] = (wide * scale).astype(jnp.bfloat16)

    def send_text(f):
        @pl.when(y < 3)
        def _():
            m_copy(f).start()

        if f < low_part:

            @pl.when(y == 3)
            def _():
                r_copy(f).start()

    def send_x(f):
        @pl.when(odd == 1)
        def _():
            x_copy(f).start()

    normalize(0, 0)
    normalize(1, 0)
    pl.semaphore_wait(barrier, 5)
    i_copy(0).start()
    send_text(0)
    normalize(1, low_part)
    send_x(low_part)
    for f in range(1, PARTS):
        normalize(0, f)
        i_copy(f).start()
        if f != low_part:
            normalize(1, f)
        send_text(f)
        if f > low_part:
            send_x(f)
    for f in range(low_part):
        send_x(f)

    def weigh(c_ref, image, i0, i_rows, text, t0, t_rows, diagonal=False):
        scores = lax.dot_general(
            imgs[image, pl.ds(i0, i_rows), :], texts[text, pl.ds(t0, t_rows), :],
            (((1,), (1,)), ((), ())), preferred_element_type=jnp.float32,
        )
        weights = jax.nn.sigmoid(mult * scores + shift)
        if diagonal:
            r = lax.broadcasted_iota(jnp.int32, weights.shape, 0) + i0
            c = lax.broadcasted_iota(jnp.int32, weights.shape, 1) + t0
            weights = jnp.where(r == c, weights - 1.0, weights)
        c_ref[pl.ds(i0, i_rows), pl.ds(t0, t_rows)] = (mult * weights).astype(jnp.bfloat16)

    def to_image(c_ref, c, text, start=0, size=rows):
        return jnp.dot(
            c_ref[span(c, part), start : start + size], texts[text, start : start + size, :],
            preferred_element_type=jnp.float32,
        )

    def x_to_image(c, start=0, size=rows):
        return jnp.dot(
            c_px[span(c, part), start : start + size], texts[x_slot, start : start + size, :],
            preferred_element_type=jnp.float32,
        )

    def to_text(c_ref, c, image, start=0, size=rows):
        return lax.dot_general(
            c_ref[start : start + size, c * part : (c + 1) * part],
            imgs[image, start : start + size, :],
            (((0,), (0,)), ((), ())), preferred_element_type=jnp.float32,
        )

    weigh(c_oa, OWN, 0, half, A, 0, rows, diagonal=True)
    weigh(c_oa, OWN, half, half, A, 0, rows, diagonal=True)
    for c in range(PARTS):
        gi[span(c, part), :] = to_image(c_oa, c, A)
    for c in range(PARTS):
        gt[span(c, part), :] = to_text(c_oa, c, OWN)

    @pl.when(y == 0)
    def _():
        for f in range(low_part):
            r_copy(f).wait_recv()
            r_forward(f).start()

    @pl.when(y == 3)
    def _():
        for f in range(low_part):
            r_copy(f).wait_send()
            x_copy(f + low_part).wait_recv()
            m_copy(f + low_part, X).start()

    @pl.when(y == 1)
    def _():
        for f in range(low_part, PARTS):
            x_copy(f).wait_recv()

    def wait_pair(first, past):
        for f in range(first, past):
            i_copy(f).wait_recv()
            m_copy(f).wait_recv()

    wait_pair(0, low_part)
    weigh(c_om, OWN, 0, rows, M, 0, half)
    weigh(c_pm, PARTNER, 0, half, M, 0, half)
    weigh(c_px, PARTNER, 0, half, x_slot, half, half)
    for c in range(low_part):
        early_m[span(c, part), :] = to_text(c_om, c, OWN) + to_text(c_pm, c, PARTNER, 0, half)
        early_x[span(c, part), :] = to_text(c_px, c + low_part, PARTNER, 0, half)
        early_p[span(c, part), :] = x_to_image(c, half, half) + to_image(c_pm, c, M, 0, half)
    for c in range(PARTS):
        gi[span(c, part), :] += to_image(c_om, c, M, 0, half)

    wait_pair(low_part, PARTS)

    @pl.when(odd == 1)
    def _():
        for f in range(low_part):
            x_copy(f).wait_recv()

    def give_gp(c, value):
        gp_out[span(c, part), :] = value.astype(jnp.bfloat16)
        gp_copy(c).start()

    def give(value, out, copy, c):
        out[span(c, part), :] = value.astype(jnp.bfloat16)
        for f in range(c * per, (c + 1) * per):
            copy(f).start()

    def give_gm(c, value):
        gm_out[span(c, part), :] = value.astype(jnp.bfloat16)

        @pl.when(jnp.logical_or(y > 0, c < low_part))
        def _():
            for f in range(c * per, (c + 1) * per):
                gm_copy(f).start()

    def give_gx(c, value):
        give(value, gx_out, lambda f: gx_copy(f, gx_out), c)

    def late_m(c):
        return early_m[span(c, part), :] + to_text(c_pm, c, PARTNER, half, half)

    def late_x(c):
        return early_x[span(c - low_part, part), :] + to_text(c_px, c, PARTNER, half, half)

    def late_p(c):
        return early_p[span(c, part), :] + x_to_image(c, 0, half) + to_image(c_pm, c, M, half, half)

    weigh(c_pm, PARTNER, half, half, M, 0, half)
    give_gm(0, late_m(0))
    weigh(c_px, PARTNER, half, half, x_slot, half, half)

    @pl.when(odd == 1)
    def _():
        give_gx(low_part, late_x(low_part))

    weigh(c_pm, PARTNER, 0, half, M, half, half)
    weigh(c_px, PARTNER, 0, half, x_slot, 0, half)
    give_gp(0, late_p(0))
    for c in range(1, low_part):
        give_gm(c, late_m(c))
        give_gp(c, late_p(c))

        @pl.when(odd == 1)
        def _():
            give_gx(low_part + c, late_x(low_part + c))

    weigh(c_om, OWN, 0, rows, M, half, half)
    weigh(c_pm, PARTNER, half, half, M, half, half)
    weigh(c_px, PARTNER, half, half, x_slot, 0, half)
    for c in range(low_part, PARTS):
        give_gm(c, to_text(c_om, c, OWN) + to_text(c_pm, c, PARTNER))
        give_gp(c, x_to_image(c) + to_image(c_pm, c, M))

    @pl.when(y == 1)
    def _():
        for c in range(low_part):
            give_gx(c, to_text(c_px, c, PARTNER))

    @pl.when(y == 3)
    def _():
        for c in range(low_part):
            early_x[span(c, part), :] = to_text(c_px, c, PARTNER)

    def wide(ref, f):
        return ref[span(f), :].astype(jnp.float32)

    def relay(f):
        @pl.when(jnp.logical_and(y == 2, f < LATE))
        def _():
            gm_copy(f).wait_recv()
            gx_copy(f, gm_in).start()

        @pl.when(jnp.logical_and(y == 3, f < low))
        def _():
            gm_copy(f).wait_recv()
            gx_out[span(f), :] = (early_x[span(f), :] + wide(gm_in, f)).astype(jnp.bfloat16)
            gx_copy(f, gx_out).start()

    for c in range(PARTS):
        relay(jnp.int32(c))
        gi[span(c, part), :] += to_image(c_om, c, M, half, half)

        @pl.when(odd == 0)
        def _():
            gt[span(c, part), :] += to_text(c_px, c, PARTNER)

    @pl.when(y == 0)
    def _():
        for f in range(low):
            gm_copy(f).wait_send()
            gm_copy(f + low).start()

    def finish(which, f, grad):
        scale = scales[which, span(f), :][:, :1]
        unit = raw[which, span(f), :].astype(jnp.float32) * scale
        inner = jnp.sum(unit * grad, axis=-1, keepdims=True)

        (image_out, text_out)[which][span(f), :] = scale * (grad - unit * inner)

    def finish_image(f):
        @pl.when(lax.rem(f, per) == 0)
        def _():
            gp_copy(f // per).wait_recv()

        finish(0, f, gi[span(f), :] + wide(gp_in, f))

    def finish_text(f):
        @pl.when(jnp.logical_or(y < 2, f >= straight_in))
        def _():
            gm_copy(f).wait_recv()
            gt[span(f), :] += wide(gm_in, f)

        @pl.when(jnp.logical_and(y > 0, jnp.logical_or(y != 2, f < LATE)))
        def _():
            gx_copy(f, gx_out).wait_recv()
            gt[span(f), :] += wide(gx_in, f)

        finish(1, f, gt[span(f), :])

    @pl.loop(0, PIECES)
    def _(f):
        @pl.when(f >= PARTS)
        def _():
            relay(f)

        finish_image(f)

        @pl.when(f >= 1)
        def _():
            finish_text(f - 1)

    finish_text(jnp.int32(PIECES - 1))

    @pl.loop(0, PARTS)
    def _(f):
        i_copy(f).wait_send()
        gp_copy(f).wait_send()

        @pl.when(jnp.logical_or(y < 3, f >= low_part))
        def _():
            m_copy(f).wait_send()

        @pl.when(jnp.logical_and(y == 0, f < low_part))
        def _():
            r_forward(f).wait_send()

        @pl.when(odd == 1)
        def _():
            x_copy(f).wait_send()

    @pl.loop(0, PIECES)
    def _(f):
        @pl.when(jnp.logical_or(y > 0, f >= low))
        def _():
            gm_copy(f).wait_send()

        @pl.when(jnp.logical_and(y > 0, jnp.logical_or(y != 2, f < LATE)))
        def _():
            gx_copy(f, gx_out).wait_send()


def store(image_ref, text_ref, image_out, text_out, sem):
    size = image_ref.shape[0] // PIECES

    def copy(which, f):
        source, target = ((image_ref, image_out), (text_ref, text_out))[which]
        here = pl.ds(f * size, size)
        return pltpu.make_async_copy(source.at[here], target.at[here], sem.at[which, f])

    for f in range(PIECES):
        copy(0, f).start()
        copy(1, f).start()
    for f in range(PIECES):
        copy(0, f).wait()
        copy(1, f).wait()


def solution(mesh):
    fold_size = mesh.shape["fold"]
    total = fold_size * mesh.shape["blk"]

    def shards(picture_vectors, caption_vectors, logit_multiplier, logit_shift_term):
        rows, width = picture_vectors.shape
        block = (rows, width)
        dma = pltpu.SemaphoreType.DMA
        grads = pl.pallas_call(
            functools.partial(kernel, total, fold_size),
            out_shape=(jax.ShapeDtypeStruct(block, jnp.float32),) * 2,
            in_specs=[pl.BlockSpec(memory_space=pl.ANY)] * 2
            + [pl.BlockSpec(memory_space=pltpu.SMEM)] * 2,
            out_specs=(pl.BlockSpec(memory_space=pltpu.VMEM),) * 2,
            scratch_shapes=[
                pltpu.VMEM((2,) + block, jnp.bfloat16),
                pltpu.VMEM((2,) + block, jnp.bfloat16),
                pltpu.VMEM((3,) + block, jnp.bfloat16),
                pltpu.VMEM((rows // HALVES, width), jnp.bfloat16),
                pltpu.VMEM((2, rows, 128), jnp.float32),
            ]
            + [pltpu.VMEM((rows, rows), jnp.bfloat16)] * 4
            + [pltpu.VMEM(block, jnp.float32)] * 2
            + [pltpu.VMEM((rows // HALVES, width), jnp.float32)] * 3
            + [pltpu.VMEM(block, jnp.bfloat16)] * 6
            + [
                dma((2, PIECES)),
            ]
            + [dma((PIECES,))] * 15,
            compiler_params=pltpu.CompilerParams(
                collective_id=0, has_side_effects=True, vmem_limit_bytes=40 << 20
            ),
            cost_estimate=pl.CostEstimate(
                flops=24 * rows * rows * width,
                bytes_accessed=12 * rows * width,
                transcendentals=4 * rows * rows,
            ),
        )(
            pltpu.with_memory_space_constraint(picture_vectors, pltpu.HBM),
            pltpu.with_memory_space_constraint(caption_vectors, pltpu.HBM),
            logit_multiplier.reshape(1, 1),
            logit_shift_term.reshape(1, 1),
        )
        return pl.pallas_call(
            store,
            out_shape=(jax.ShapeDtypeStruct(block, jnp.float32),) * 2,
            in_specs=[pl.BlockSpec(memory_space=pl.ANY)] * 2,
            out_specs=(pl.BlockSpec(memory_space=pl.ANY),) * 2,
            scratch_shapes=[dma((2, PIECES))],
            compiler_params=pltpu.CompilerParams(vmem_limit_bytes=1 << 20),
        )(*grads)

    placed = (P(("blk", "fold"), None), P(("blk", "fold"), None), P(), P())
    return jax.shard_map(
        shards,
        mesh=mesh,
        in_specs=placed,
        out_specs=(P(("blk", "fold"), None), P(("blk", "fold"), None)),
        check_vma=False,
    )
```

```python
import functools

import jax
import jax.numpy as jnp
from jax import lax
from jax.experimental import pallas as pl
from jax.experimental.pallas import tpu as pltpu
from jax.sharding import PartitionSpec as P

MESH = pl.DeviceIdType.MESH
PIECES = 8
PARTS = 4
LATE = 7
LAG = 3
STORES = 2
HALVES = 2
OWN, PARTNER = 0, 1
A, M, X = 0, 1, 2


def kernel(
    total, fold_size, image_ref, text_ref, mult_ref, shift_ref, image_out, text_out,
    raw, imgs, texts, passing, scales, c_oa, c_px, c_om, c_pm, gi, gt, early_m, early_x, early_p,
    gp_out, gm_out, gx_out, gp_in, gm_in, gx_in,
    load_sem, i_send, i_recv, m_send, m_recv, x_send, x_recv, r_send, r_recv, fw_send,
    gp_send, gp_recv, gm_send, gm_recv, gx_send, gx_recv,
):
    rows, width = raw.shape[1:]
    piece, part, half = rows // PIECES, rows // PARTS, rows // HALVES
    low = PIECES // HALVES
    low_part = PARTS // HALVES
    per = PIECES // PARTS
    d = lax.axis_index("blk") * fold_size + lax.axis_index("fold")
    y = lax.rem(d, 4)
    odd = lax.rem(y, 2)
    x_slot = 2 * odd
    mult, shift = mult_ref[0, 0], shift_ref[0, 0]

    def device(number):
        number = lax.rem(number + total, total)
        return (number // fold_size, lax.rem(number, fold_size))

    def where(*values):
        picked = jnp.int32(values[0])
        for place in range(1, 4):
            picked = jnp.where(y == place, jnp.int32(values[place]), picked)
        return picked

    def span(f, size=None):
        size = piece if size is None else size
        return pl.ds(pl.multiple_of(f * size, size), size)

    partner = device(d + 1 - 2 * odd)

    def remote(src, dst, send, recv, target):
        return pltpu.make_async_remote_copy(
            src_ref=src, dst_ref=dst, send_sem=send, recv_sem=recv,
            device_id=target, device_id_type=MESH,
        )

    def i_copy(f):
        return remote(
            imgs.at[OWN, span(f, part)], imgs.at[PARTNER, span(f, part)], i_send.at[f], i_recv.at[f], partner
        )

    def m_copy(f, slot=A):
        return remote(
            texts.at[slot, span(f, part)], texts.at[M, span(f, part)], m_send.at[f], m_recv.at[f],
            device(d + where(3, 1, 3, -3)),
        )

    def x_copy(f):
        return remote(
            texts.at[A, span(f, part)], texts.at[X, span(f, part)], x_send.at[f], x_recv.at[f], device(d + 4)
        )

    def r_copy(f):
        return remote(
            texts.at[A, span(f, part)], passing.at[span(f, part)], r_send.at[f], r_recv.at[f], device(d - 3)
        )

    def r_forward(f):
        return remote(
            passing.at[span(f, part)], texts.at[M, span(f, part)], fw_send.at[f], m_recv.at[f], device(d + 4)
        )

    def gp_copy(f):
        return remote(gp_out.at[span(f, part)], gp_in.at[span(f, part)], gp_send.at[f], gp_recv.at[f], partner)

    n_handed = low
    straight_in = where(PIECES, PIECES, LATE, n_handed)

    def gm_copy(f):
        step = jnp.where(jnp.logical_and(y == 1, f >= LATE), -3, where(-1, 1, -1, -3))
        return remote(
            gm_out.at[span(f)], gm_in.at[span(f)], gm_send.at[f], gm_recv.at[f], device(d + step)
        )

    def hand_copy(f):
        return remote(
            gm_out.at[span(f)], passing.at[span(f)], gm_send.at[f], r_recv.at[f], device(d + 3)
        )

    def gx_copy(f, source):
        return remote(
            source.at[span(f)], gx_in.at[span(f)], gx_send.at[f], gx_recv.at[f], device(d - 4)
        )

    def load(which, f):
        source = (image_ref, text_ref)[which]
        return pltpu.make_async_copy(
            source.at[span(f, part)], raw.at[which, span(f, part)], load_sem.at[which, f]
        )

    barrier = pltpu.get_barrier_semaphore()
    near = {0: (1, 3, 4, -4, -1), 1: (-1, 1, 4, -4, -3), 2: (1, 3, -1, 4, -4), 3: (-1, -3, 4, -4, 1)}
    for place, offsets in near.items():

        @pl.when(y == place)
        def _():
            for offset in offsets:
                pl.semaphore_signal(
                    barrier, inc=1, device_id=device(d + offset), device_id_type=MESH
                )

    for f in range(PARTS):
        load(0, f).start()
        load(1, f).start()

    def normalize(which, f):
        load(which, f).wait()
        here = span(f, part)
        wide = raw[which, here, :].astype(jnp.float32)
        scale = 1.0 / jnp.sqrt(jnp.sum(wide * wide, axis=-1, keepdims=True) + 1e-06)
        scales[which, here, :] = jnp.broadcast_to(scale, (part, scales.shape[-1]))
        (imgs, texts)[which][0, here, :] = (wide * scale).astype(jnp.bfloat16)

    def send_text(f):
        @pl.when(y < 3)
        def _():
            m_copy(f).start()

        if f < low_part:

            @pl.when(y == 3)
            def _():
                r_copy(f).start()

    def send_x(f):
        @pl.when(odd == 1)
        def _():
            x_copy(f).start()

    normalize(0, 0)
    pl.semaphore_wait(barrier, 5)
    i_copy(0).start()
    normalize(1, 0)
    send_text(0)
    normalize(1, low_part)
    send_x(low_part)
    for f in range(1, PARTS):
        normalize(0, f)
        i_copy(f).start()
        if f != low_part:
            normalize(1, f)
        send_text(f)
        if f > low_part:
            send_x(f)
    for f in range(low_part):
        send_x(f)

    def weigh(c_ref, image, i0, i_rows, text, t0, t_rows, diagonal=False):
        scores = lax.dot_general(
            imgs[image, pl.ds(i0, i_rows), :], texts[text, pl.ds(t0, t_rows), :],
            (((1,), (1,)), ((), ())), preferred_element_type=jnp.float32,
        )
        weights = jax.nn.sigmoid(mult * scores + shift)
        if diagonal:
            r = lax.broadcasted_iota(jnp.int32, weights.shape, 0) + i0
            c = lax.broadcasted_iota(jnp.int32, weights.shape, 1) + t0
            weights = jnp.where(r == c, weights - 1.0, weights)
        c_ref[pl.ds(i0, i_rows), pl.ds(t0, t_rows)] = (mult * weights).astype(jnp.bfloat16)

    def to_image(c_ref, c, text, start=0, size=rows):
        return jnp.dot(
            c_ref[span(c, part), start : start + size], texts[text, start : start + size, :],
            preferred_element_type=jnp.float32,
        )

    def x_to_image(c, start=0, size=rows):
        return jnp.dot(
            c_px[span(c, part), start : start + size], texts[x_slot, start : start + size, :],
            preferred_element_type=jnp.float32,
        )

    def to_text(c_ref, c, image, start=0, size=rows):
        return lax.dot_general(
            c_ref[start : start + size, c * part : (c + 1) * part],
            imgs[image, start : start + size, :],
            (((0,), (0,)), ((), ())), preferred_element_type=jnp.float32,
        )

    weigh(c_oa, OWN, 0, half, A, 0, rows, diagonal=True)
    weigh(c_oa, OWN, half, half, A, 0, rows, diagonal=True)
    for c in range(PARTS):
        gi[span(c, part), :] = to_image(c_oa, c, A)
    for c in range(PARTS):
        gt[span(c, part), :] = to_text(c_oa, c, OWN)

    @pl.when(y == 0)
    def _():
        for f in range(low_part):
            r_copy(f).wait_recv()
            r_forward(f).start()

    @pl.when(y == 3)
    def _():
        for f in range(low_part):
            r_copy(f).wait_send()
            x_copy(f + low_part).wait_recv()
            m_copy(f + low_part, X).start()

    @pl.when(y == 1)
    def _():
        for f in range(low_part, PARTS):
            x_copy(f).wait_recv()

    for f in range(low_part):
        i_copy(f).wait_recv()
        m_copy(f).wait_recv()
    weigh(c_om, OWN, 0, rows, M, 0, half)
    weigh(c_pm, PARTNER, 0, half, M, 0, half)
    weigh(c_px, PARTNER, 0, half, x_slot, half, half)
    for c in range(low_part):
        early_m[span(c, part), :] = to_text(c_om, c, OWN) + to_text(c_pm, c, PARTNER, 0, half)
        early_x[span(c, part), :] = to_text(c_px, c + low_part, PARTNER, 0, half)
        early_p[span(c, part), :] = x_to_image(c, half, half) + to_image(c_pm, c, M, 0, half)
    for c in range(PARTS):
        gi[span(c, part), :] += to_image(c_om, c, M, 0, half)

    def give_gp(c, value):
        gp_out[span(c, part), :] = value.astype(jnp.bfloat16)
        gp_copy(c).start()

    def give(value, out, copy, c):
        out[span(c, part), :] = value.astype(jnp.bfloat16)
        for f in range(c * per, (c + 1) * per):
            copy(f).start()

    def give_gm(c, value):
        gm_out[span(c, part), :] = value.astype(jnp.bfloat16)

        for f in range(c * per, (c + 1) * per):
            by_hand = jnp.logical_and(y == 0, f < n_handed)

            @pl.when(by_hand)
            def _():
                hand_copy(f).start()

            @pl.when(jnp.logical_not(by_hand))
            def _():
                gm_copy(f).start()

    def give_gx(c, value):
        give(value, gx_out, lambda f: gx_copy(f, gx_out), c)

    def late_m(c):
        return early_m[span(c, part), :] + to_text(c_pm, c, PARTNER, half, half)

    def late_x(c):
        return early_x[span(c - low_part, part), :] + to_text(c_px, c, PARTNER, half, half)

    def late_p(c):
        return early_p[span(c, part), :] + x_to_image(c, 0, half) + to_image(c_pm, c, M, half, half)

    for f in range(low_part, PARTS):
        i_copy(f).wait_recv()
    weigh(c_pm, PARTNER, half, half, M, 0, half)
    give_gm(0, late_m(0))
    weigh(c_px, PARTNER, half, half, x_slot, half, half)

    @pl.when(odd == 1)
    def _():
        give_gx(low_part, late_x(low_part))

    for f in range(low_part, PARTS):
        m_copy(f).wait_recv()

    @pl.when(odd == 1)
    def _():
        for f in range(low_part):
            x_copy(f).wait_recv()

    weigh(c_pm, PARTNER, 0, half, M, half, half)
    weigh(c_px, PARTNER, 0, half, x_slot, 0, half)
    give_gp(0, late_p(0))
    for c in range(1, low_part):
        give_gm(c, late_m(c))
        give_gp(c, late_p(c))

        @pl.when(odd == 1)
        def _():
            give_gx(low_part + c, late_x(low_part + c))

    weigh(c_om, OWN, 0, rows, M, half, half)
    weigh(c_pm, PARTNER, half, half, M, half, half)
    weigh(c_px, PARTNER, half, half, x_slot, 0, half)
    for c in range(low_part, PARTS):
        give_gm(c, to_text(c_om, c, OWN) + to_text(c_pm, c, PARTNER))
        give_gp(c, x_to_image(c) + to_image(c_pm, c, M))

    @pl.when(odd == 1)
    def _():
        for c in range(low_part):
            value = to_text(c_px, c, PARTNER)
            early_x[span(c, part), :] = value
            gx_out[span(c, part), :] = value.astype(jnp.bfloat16)
            for f in range(c * per, (c + 1) * per):

                @pl.when(jnp.logical_or(y == 1, f >= n_handed))
                def _():
                    gx_copy(f, gx_out).start()

    def wide(ref, f):
        return ref[span(f), :].astype(jnp.float32)

    def relay(f):
        @pl.when(jnp.logical_and(y == 2, f < LATE))
        def _():
            gm_copy(f).wait_recv()
            gx_copy(f, gm_in).start()

        @pl.when(jnp.logical_and(y == 3, f < n_handed))
        def _():
            hand_copy(f).wait_recv()
            gx_out[span(f), :] = (early_x[span(f), :] + wide(passing, f)).astype(jnp.bfloat16)
            gx_copy(f, gx_out).start()

    for c in range(PARTS):
        relay(jnp.int32(c))
        gi[span(c, part), :] += to_image(c_om, c, M, half, half)

        @pl.when(odd == 0)
        def _():
            gt[span(c, part), :] += to_text(c_px, c, PARTNER)

    def finish(which, f, grad):
        scale = scales[which, span(f), :][:, :1]
        unit = raw[which, span(f), :].astype(jnp.float32) * scale
        inner = jnp.sum(unit * grad, axis=-1, keepdims=True)

        (image_out, text_out)[which][span(f), :] = scale * (grad - unit * inner)

    def finish_image(f):
        @pl.when(lax.rem(f, per) == 0)
        def _():
            gp_copy(f // per).wait_recv()

        finish(0, f, gi[span(f), :] + wide(gp_in, f))

    def finish_text(f):
        @pl.when(jnp.logical_or(y < 2, f >= straight_in))
        def _():
            gm_copy(f).wait_recv()
            gt[span(f), :] += wide(gm_in, f)

        @pl.when(jnp.logical_and(y > 0, jnp.logical_or(y != 2, f < LATE)))
        def _():
            gx_copy(f, gx_out).wait_recv()
            gt[span(f), :] += wide(gx_in, f)

        finish(1, f, gt[span(f), :])

    def text_order(k):
        return jnp.where(y == 2, k, lax.div(k, 2) + low * lax.rem(k, 2))

    @pl.loop(0, PIECES + LAG)
    def _(f):
        @pl.when(jnp.logical_and(f >= PARTS, f < PIECES))
        def _():
            relay(f)

        @pl.when(f >= LAG)
        def _():
            finish_image(f - LAG)
            finish_text(text_order(f - LAG))

    @pl.loop(0, PARTS)
    def _(f):
        i_copy(f).wait_send()
        gp_copy(f).wait_send()

        @pl.when(jnp.logical_or(y < 3, f >= low_part))
        def _():
            m_copy(f).wait_send()

        @pl.when(jnp.logical_and(y == 0, f < low_part))
        def _():
            r_forward(f).wait_send()

        @pl.when(odd == 1)
        def _():
            x_copy(f).wait_send()

    @pl.loop(0, PIECES)
    def _(f):
        gm_copy(f).wait_send()

        @pl.when(jnp.logical_and(y > 0, jnp.logical_or(y != 2, f < LATE)))
        def _():
            gx_copy(f, gx_out).wait_send()


def store(image_ref, text_ref, image_out, text_out, sem):
    size = image_ref.shape[0] // STORES

    def copy(which, f):
        source, target = ((image_ref, image_out), (text_ref, text_out))[which]
        here = pl.ds(f * size, size)
        return pltpu.make_async_copy(source.at[here], target.at[here], sem.at[which, f])

    for f in range(STORES):
        copy(0, f).start()
        copy(1, f).start()
    for f in range(STORES):
        copy(0, f).wait()
        copy(1, f).wait()


def solution(mesh):
    fold_size = mesh.shape["fold"]
    total = fold_size * mesh.shape["blk"]

    def shards(picture_vectors, caption_vectors, logit_multiplier, logit_shift_term):
        rows, width = picture_vectors.shape
        block = (rows, width)
        dma = pltpu.SemaphoreType.DMA
        grads = pl.pallas_call(
            functools.partial(kernel, total, fold_size),
            out_shape=(jax.ShapeDtypeStruct(block, jnp.float32),) * 2,
            in_specs=[pl.BlockSpec(memory_space=pl.ANY)] * 2
            + [pl.BlockSpec(memory_space=pltpu.SMEM)] * 2,
            out_specs=(pl.BlockSpec(memory_space=pltpu.VMEM),) * 2,
            scratch_shapes=[
                pltpu.VMEM((2,) + block, jnp.bfloat16),
                pltpu.VMEM((2,) + block, jnp.bfloat16),
                pltpu.VMEM((3,) + block, jnp.bfloat16),
                pltpu.VMEM((rows // HALVES, width), jnp.bfloat16),
                pltpu.VMEM((2, rows, 128), jnp.float32),
            ]
            + [pltpu.VMEM((rows, rows), jnp.bfloat16)] * 4
            + [pltpu.VMEM(block, jnp.float32)] * 2
            + [pltpu.VMEM((rows // HALVES, width), jnp.float32)] * 3
            + [pltpu.VMEM(block, jnp.bfloat16)] * 6
            + [
                dma((2, PIECES)),
            ]
            + [dma((PIECES,))] * 15,
            compiler_params=pltpu.CompilerParams(
                collective_id=0, has_side_effects=True, vmem_limit_bytes=40 << 20
            ),
            cost_estimate=pl.CostEstimate(
                flops=24 * rows * rows * width,
                bytes_accessed=12 * rows * width,
                transcendentals=4 * rows * rows,
            ),
        )(
            pltpu.with_memory_space_constraint(picture_vectors, pltpu.HBM),
            pltpu.with_memory_space_constraint(caption_vectors, pltpu.HBM),
            logit_multiplier.reshape(1, 1),
            logit_shift_term.reshape(1, 1),
        )
        return pl.pallas_call(
            store,
            out_shape=(jax.ShapeDtypeStruct(block, jnp.float32),) * 2,
            in_specs=[pl.BlockSpec(memory_space=pl.ANY)] * 2,
            out_specs=(pl.BlockSpec(memory_space=pl.ANY),) * 2,
            scratch_shapes=[dma((2, STORES))],
            compiler_params=pltpu.CompilerParams(vmem_limit_bytes=1 << 20),
        )(*grads)

    placed = (P(("blk", "fold"), None), P(("blk", "fold"), None), P(), P())
    return jax.shard_map(
        shards,
        mesh=mesh,
        in_specs=placed,
        out_specs=(P(("blk", "fold"), None), P(("blk", "fold"), None)),
        check_vma=False,
    )
```

```python
import functools

import jax
import jax.numpy as jnp
from jax import lax
from jax.experimental import pallas as pl
from jax.experimental.pallas import tpu as pltpu
from jax.sharding import PartitionSpec as P

MESH = pl.DeviceIdType.MESH
PIECES = 8
PARTS = 4
LATE = 7
LAG = 3
STORES = 2
HALVES = 2
OWN, PARTNER = 0, 1
A, M, X = 0, 1, 2


def kernel(
    total, fold_size, image_ref, text_ref, mult_ref, shift_ref, image_out, text_out,
    raw, imgs, texts, passing, scales, c_oa, c_px, c_om, c_pm, gi, gt, early_m, early_x, early_p,
    gp_out, gm_out, gx_out, gp_in, gm_in, gx_in,
    load_sem, i_send, i_recv, m_send, m_recv, x_send, x_recv, r_send, r_recv, fw_send,
    gp_send, gp_recv, gm_send, gm_recv, gx_send, gx_recv,
):
    rows, width = raw.shape[1:]
    piece, part, half = rows // PIECES, rows // PARTS, rows // HALVES
    low = PIECES // HALVES
    low_part = PARTS // HALVES
    per = PIECES // PARTS
    d = lax.axis_index("blk") * fold_size + lax.axis_index("fold")
    y = lax.rem(d, 4)
    odd = lax.rem(y, 2)
    x_slot = 2 * odd
    mult, shift = mult_ref[0, 0], shift_ref[0, 0]

    def device(number):
        number = lax.rem(number + total, total)
        return (number // fold_size, lax.rem(number, fold_size))

    def where(*values):
        picked = jnp.int32(values[0])
        for place in range(1, 4):
            picked = jnp.where(y == place, jnp.int32(values[place]), picked)
        return picked

    def span(f, size=None):
        size = piece if size is None else size
        return pl.ds(pl.multiple_of(f * size, size), size)

    partner = device(d + 1 - 2 * odd)

    def remote(src, dst, send, recv, target):
        return pltpu.make_async_remote_copy(
            src_ref=src, dst_ref=dst, send_sem=send, recv_sem=recv,
            device_id=target, device_id_type=MESH,
        )

    def i_copy(f):
        return remote(
            imgs.at[OWN, span(f, part)], imgs.at[PARTNER, span(f, part)], i_send.at[f], i_recv.at[f], partner
        )

    def m_copy(f, slot=A):
        return remote(
            texts.at[slot, span(f, part)], texts.at[M, span(f, part)], m_send.at[f], m_recv.at[f],
            device(d + where(3, 1, 3, -3)),
        )

    def x_copy(f):
        return remote(
            texts.at[A, span(f, part)], texts.at[X, span(f, part)], x_send.at[f], x_recv.at[f], device(d + 4)
        )

    def r_copy(f):
        return remote(
            texts.at[A, span(f, part)], passing.at[span(f, part)], r_send.at[f], r_recv.at[f], device(d - 3)
        )

    def r_forward(f):
        return remote(
            passing.at[span(f, part)], texts.at[M, span(f, part)], fw_send.at[f], m_recv.at[f], device(d + 4)
        )

    def gp_copy(f):
        return remote(gp_out.at[span(f, part)], gp_in.at[span(f, part)], gp_send.at[f], gp_recv.at[f], partner)

    n_handed = low
    straight_in = where(PIECES, PIECES, LATE, n_handed)

    def gm_copy(f):
        step = jnp.where(jnp.logical_and(y == 1, f >= LATE), -3, where(-1, 1, -1, -3))
        return remote(
            gm_out.at[span(f)], gm_in.at[span(f)], gm_send.at[f], gm_recv.at[f], device(d + step)
        )

    def hand_copy(f):
        return remote(
            gm_out.at[span(f)], passing.at[span(f)], gm_send.at[f], r_recv.at[f], device(d + 3)
        )

    def gx_copy(f, source):
        return remote(
            source.at[span(f)], gx_in.at[span(f)], gx_send.at[f], gx_recv.at[f], device(d - 4)
        )

    def load(which, f):
        source = (image_ref, text_ref)[which]
        return pltpu.make_async_copy(
            source.at[span(f, part)], raw.at[which, span(f, part)], load_sem.at[which, f]
        )

    barrier = pltpu.get_barrier_semaphore()
    near = {0: (1, 3, 4, -4, -1), 1: (-1, 1, 4, -4, -3), 2: (1, 3, -1, 4, -4), 3: (-1, -3, 4, -4, 1)}
    for place, offsets in near.items():

        @pl.when(y == place)
        def _():
            for offset in offsets:
                pl.semaphore_signal(
                    barrier, inc=1, device_id=device(d + offset), device_id_type=MESH
                )

    for f in range(PARTS):
        load(0, f).start()
        load(1, f).start()

    def normalize(which, f):
        load(which, f).wait()
        here = span(f, part)
        wide = raw[which, here, :].astype(jnp.float32)
        scale = 1.0 / jnp.sqrt(jnp.sum(wide * wide, axis=-1, keepdims=True) + 1e-06)
        scales[which, here, :] = jnp.broadcast_to(scale, (part, scales.shape[-1]))
        (imgs, texts)[which][0, here, :] = (wide * scale).astype(jnp.bfloat16)

    def send_text(f):
        @pl.when(y < 3)
        def _():
            m_copy(f).start()

        if f < low_part:

            @pl.when(y == 3)
            def _():
                r_copy(f).start()

    def send_x(f):
        @pl.when(odd == 1)
        def _():
            x_copy(f).start()

    normalize(0, 0)
    pl.semaphore_wait(barrier, 5)
    i_copy(0).start()
    normalize(1, 0)
    send_text(0)
    normalize(1, low_part)
    send_x(low_part)
    for f in range(1, PARTS):
        normalize(0, f)
        i_copy(f).start()
        if f != low_part:
            normalize(1, f)
        send_text(f)
        if f > low_part:
            send_x(f)
    for f in range(low_part):
        send_x(f)

    def weigh(c_ref, image, i0, i_rows, text, t0, t_rows, diagonal=False):
        scores = lax.dot_general(
            imgs[image, pl.ds(i0, i_rows), :], texts[text, pl.ds(t0, t_rows), :],
            (((1,), (1,)), ((), ())), preferred_element_type=jnp.float32,
        )
        weights = jax.nn.sigmoid(mult * scores + shift)
        if diagonal:
            r = lax.broadcasted_iota(jnp.int32, weights.shape, 0) + i0
            c = lax.broadcasted_iota(jnp.int32, weights.shape, 1) + t0
            weights = jnp.where(r == c, weights - 1.0, weights)
        c_ref[pl.ds(i0, i_rows), pl.ds(t0, t_rows)] = (mult * weights).astype(jnp.bfloat16)

    def to_image(c_ref, c, text, start=0, size=rows):
        return jnp.dot(
            c_ref[span(c, part), start : start + size], texts[text, start : start + size, :],
            preferred_element_type=jnp.float32,
        )

    def x_to_image(c, start=0, size=rows):
        return jnp.dot(
            c_px[span(c, part), start : start + size], texts[x_slot, start : start + size, :],
            preferred_element_type=jnp.float32,
        )

    def to_text(c_ref, c, image, start=0, size=rows):
        return lax.dot_general(
            c_ref[start : start + size, c * part : (c + 1) * part],
            imgs[image, start : start + size, :],
            (((0,), (0,)), ((), ())), preferred_element_type=jnp.float32,
        )

    weigh(c_oa, OWN, 0, half, A, 0, rows, diagonal=True)
    weigh(c_oa, OWN, half, half, A, 0, rows, diagonal=True)
    for c in range(PARTS):
        gi[span(c, part), :] = to_image(c_oa, c, A)
    for c in range(PARTS):
        gt[span(c, part), :] = to_text(c_oa, c, OWN)

    @pl.when(y == 0)
    def _():
        for f in range(low_part):
            r_copy(f).wait_recv()
            r_forward(f).start()

    @pl.when(y == 3)
    def _():
        for f in range(low_part):
            r_copy(f).wait_send()
            x_copy(f + low_part).wait_recv()
            m_copy(f + low_part, X).start()

    @pl.when(y == 1)
    def _():
        for f in range(low_part, PARTS):
            x_copy(f).wait_recv()

    for f in range(low_part):
        i_copy(f).wait_recv()
        m_copy(f).wait_recv()
    weigh(c_om, OWN, 0, rows, M, 0, half)
    weigh(c_pm, PARTNER, 0, half, M, 0, half)
    weigh(c_px, PARTNER, 0, half, x_slot, half, half)
    for c in range(low_part):
        early_m[span(c, part), :] = to_text(c_om, c, OWN) + to_text(c_pm, c, PARTNER, 0, half)
        early_x[span(c, part), :] = to_text(c_px, c + low_part, PARTNER, 0, half)
        early_p[span(c, part), :] = x_to_image(c, half, half) + to_image(c_pm, c, M, 0, half)
    for c in range(PARTS):
        gi[span(c, part), :] += to_image(c_om, c, M, 0, half)

    def give_gp(c, value):
        gp_out[span(c, part), :] = value.astype(jnp.bfloat16)
        gp_copy(c).start()

    def give(value, out, copy, c):
        out[span(c, part), :] = value.astype(jnp.bfloat16)
        for f in range(c * per, (c + 1) * per):
            copy(f).start()

    def give_gm(c, value):
        gm_out[span(c, part), :] = value.astype(jnp.bfloat16)

        for f in range(c * per, (c + 1) * per):
            by_hand = jnp.logical_and(y == 0, f < n_handed)

            @pl.when(by_hand)
            def _():
                hand_copy(f).start()

            @pl.when(y > (1 if f == LATE else 0))
            def _():
                gm_copy(f).start()

    def give_gx(c, value):
        give(value, gx_out, lambda f: gx_copy(f, gx_out), c)

    def late_m(c):
        return early_m[span(c, part), :] + to_text(c_pm, c, PARTNER, half, half)

    def late_x(c):
        return early_x[span(c - low_part, part), :] + to_text(c_px, c, PARTNER, half, half)

    def late_p(c):
        return early_p[span(c, part), :] + x_to_image(c, 0, half) + to_image(c_pm, c, M, half, half)

    for f in range(low_part, PARTS):
        i_copy(f).wait_recv()
    weigh(c_pm, PARTNER, half, half, M, 0, half)
    give_gm(0, late_m(0))
    weigh(c_px, PARTNER, half, half, x_slot, half, half)

    @pl.when(odd == 1)
    def _():
        give_gx(low_part, late_x(low_part))

    for f in range(low_part, PARTS):
        m_copy(f).wait_recv()

    @pl.when(odd == 1)
    def _():
        for f in range(low_part):
            x_copy(f).wait_recv()

    weigh(c_pm, PARTNER, 0, half, M, half, half)
    weigh(c_px, PARTNER, 0, half, x_slot, 0, half)
    give_gp(0, late_p(0))
    for c in range(1, low_part):
        give_gm(c, late_m(c))
        give_gp(c, late_p(c))

        @pl.when(odd == 1)
        def _():
            give_gx(low_part + c, late_x(low_part + c))

    weigh(c_om, OWN, 0, rows, M, half, half)
    weigh(c_pm, PARTNER, half, half, M, half, half)
    weigh(c_px, PARTNER, half, half, x_slot, 0, half)
    for c in range(low_part, PARTS):
        give_gm(c, to_text(c_om, c, OWN) + to_text(c_pm, c, PARTNER))
        give_gp(c, x_to_image(c) + to_image(c_pm, c, M))

    @pl.when(odd == 1)
    def _():
        for c in range(low_part):
            value = to_text(c_px, c, PARTNER)
            early_x[span(c, part), :] = value
            gx_out[span(c, part), :] = value.astype(jnp.bfloat16)
            for f in range(c * per, (c + 1) * per):

                @pl.when(jnp.logical_or(y == 1, f >= n_handed))
                def _():
                    gx_copy(f, gx_out).start()

    def wide(ref, f):
        return ref[span(f), :].astype(jnp.float32)

    def relay(f):
        @pl.when(jnp.logical_and(y == 2, f < LATE))
        def _():
            gm_copy(f).wait_recv()
            gx_copy(f, gm_in).start()

        @pl.when(jnp.logical_and(y == 3, f < n_handed))
        def _():
            hand_copy(f).wait_recv()
            gx_out[span(f), :] = (early_x[span(f), :] + wide(passing, f)).astype(jnp.bfloat16)
            gx_copy(f, gx_out).start()

    for c in range(PARTS):
        relay(jnp.int32(c))
        gi[span(c, part), :] += to_image(c_om, c, M, half, half)

        @pl.when(odd == 0)
        def _():
            gt[span(c, part), :] += to_text(c_px, c, PARTNER)

    @pl.when(y == 0)
    def _():
        for f in range(n_handed):
            hand_copy(f).wait_send()
            gm_copy(f + n_handed).start()

    def finish(which, f, grad):
        scale = scales[which, span(f), :][:, :1]
        unit = raw[which, span(f), :].astype(jnp.float32) * scale
        inner = jnp.sum(unit * grad, axis=-1, keepdims=True)

        (image_out, text_out)[which][span(f), :] = scale * (grad - unit * inner)

    def finish_image(f):
        @pl.when(lax.rem(f, per) == 0)
        def _():
            gp_copy(f // per).wait_recv()

        finish(0, f, gi[span(f), :] + wide(gp_in, f))

    def finish_text(f):
        @pl.when(jnp.logical_or(y < 2, f >= straight_in))
        def _():
            gm_copy(f).wait_recv()
            gt[span(f), :] += wide(gm_in, f)

        @pl.when(jnp.logical_and(y > 0, jnp.logical_or(y != 2, f < LATE)))
        def _():
            gx_copy(f, gx_out).wait_recv()
            gt[span(f), :] += wide(gx_in, f)

        finish(1, f, gt[span(f), :])

    def text_order(k):
        return jnp.where(y == 2, k, lax.div(k, 2) + low * lax.rem(k, 2))

    @pl.loop(0, PIECES + LAG)
    def _(f):
        @pl.when(jnp.logical_and(f >= PARTS, f < PIECES))
        def _():
            relay(f)

        @pl.when(jnp.logical_and(y == 1, f == PIECES - 1))
        def _():
            gm_copy(LATE - 2).wait_send()
            gm_copy(LATE).start()

        @pl.when(f >= LAG)
        def _():
            finish_image(f - LAG)
            finish_text(text_order(f - LAG))

    @pl.loop(0, PARTS)
    def _(f):
        i_copy(f).wait_send()
        gp_copy(f).wait_send()

        @pl.when(jnp.logical_or(y < 3, f >= low_part))
        def _():
            m_copy(f).wait_send()

        @pl.when(jnp.logical_and(y == 0, f < low_part))
        def _():
            r_forward(f).wait_send()

        @pl.when(odd == 1)
        def _():
            x_copy(f).wait_send()

    @pl.loop(0, PIECES)
    def _(f):
        @pl.when(jnp.where(y == 0, f >= n_handed, jnp.logical_or(y > 1, f != LATE - 2)))
        def _():
            gm_copy(f).wait_send()

        @pl.when(jnp.logical_and(y > 0, jnp.logical_or(y != 2, f < LATE)))
        def _():
            gx_copy(f, gx_out).wait_send()


def store(image_ref, text_ref, image_out, text_out, sem):
    size = image_ref.shape[0] // STORES

    def copy(which, f):
        source, target = ((image_ref, image_out), (text_ref, text_out))[which]
        here = pl.ds(f * size, size)
        return pltpu.make_async_copy(source.at[here], target.at[here], sem.at[which, f])

    for f in range(STORES):
        copy(0, f).start()
        copy(1, f).start()
    for f in range(STORES):
        copy(0, f).wait()
        copy(1, f).wait()


def solution(mesh):
    fold_size = mesh.shape["fold"]
    total = fold_size * mesh.shape["blk"]

    def shards(picture_vectors, caption_vectors, logit_multiplier, logit_shift_term):
        rows, width = picture_vectors.shape
        block = (rows, width)
        dma = pltpu.SemaphoreType.DMA
        grads = pl.pallas_call(
            functools.partial(kernel, total, fold_size),
            out_shape=(jax.ShapeDtypeStruct(block, jnp.float32),) * 2,
            in_specs=[pl.BlockSpec(memory_space=pl.ANY)] * 2
            + [pl.BlockSpec(memory_space=pltpu.SMEM)] * 2,
            out_specs=(pl.BlockSpec(memory_space=pltpu.VMEM),) * 2,
            scratch_shapes=[
                pltpu.VMEM((2,) + block, jnp.bfloat16),
                pltpu.VMEM((2,) + block, jnp.bfloat16),
                pltpu.VMEM((3,) + block, jnp.bfloat16),
                pltpu.VMEM((rows // HALVES, width), jnp.bfloat16),
                pltpu.VMEM((2, rows, 128), jnp.float32),
            ]
            + [pltpu.VMEM((rows, rows), jnp.bfloat16)] * 4
            + [pltpu.VMEM(block, jnp.float32)] * 2
            + [pltpu.VMEM((rows // HALVES, width), jnp.float32)] * 3
            + [pltpu.VMEM(block, jnp.bfloat16)] * 6
            + [
                dma((2, PIECES)),
            ]
            + [dma((PIECES,))] * 15,
            compiler_params=pltpu.CompilerParams(
                collective_id=0, has_side_effects=True, vmem_limit_bytes=40 << 20
            ),
            cost_estimate=pl.CostEstimate(
                flops=24 * rows * rows * width,
                bytes_accessed=12 * rows * width,
                transcendentals=4 * rows * rows,
            ),
        )(
            pltpu.with_memory_space_constraint(picture_vectors, pltpu.HBM),
            pltpu.with_memory_space_constraint(caption_vectors, pltpu.HBM),
            logit_multiplier.reshape(1, 1),
            logit_shift_term.reshape(1, 1),
        )
        return pl.pallas_call(
            store,
            out_shape=(jax.ShapeDtypeStruct(block, jnp.float32),) * 2,
            in_specs=[pl.BlockSpec(memory_space=pl.ANY)] * 2,
            out_specs=(pl.BlockSpec(memory_space=pl.ANY),) * 2,
            scratch_shapes=[dma((2, STORES))],
            compiler_params=pltpu.CompilerParams(vmem_limit_bytes=1 << 20),
        )(*grads)

    placed = (P(("blk", "fold"), None), P(("blk", "fold"), None), P(), P())
    return jax.shard_map(
        shards,
        mesh=mesh,
        in_specs=placed,
        out_specs=(P(("blk", "fold"), None), P(("blk", "fold"), None)),
        check_vma=False,
    )
```
